128 devices in a mesh: ctx: 8 (over z, core), tp: 16 (over y, x).
Axes of the slice: x: 4, y: 4, z: 4, core: 2. Of those that a mesh axis runs over, the one named last changes fastest.
Arguments:
- query: bfloat16 [8192, 16384], P('ctx', 'tp'), may hold values from -9 to 9
- keys: bfloat16 [8192, 1024], P('ctx'), may hold values from -9 to 9
- values: bfloat16 [8192, 1024], P('ctx'), may hold values from -6 to 6
- d_out: bfloat16 [8192, 16384], P('ctx', 'tp'), may hold values from -6 to 6
- inputs: bfloat16 [8192, 16384], P('ctx', 'tp'), may hold values from -72 to 72
- kv_weight: float32 [2048, 16384], P('ctx', 'tp'), may hold values from -40 to 40
- moment: float32 [2048, 16384], P('ctx', 'tp'), may hold values from -240 to 240
- velocity: float32 [2048, 16384], P('ctx', 'tp'), may hold values from 0.3 to 30
- doc_lengths: int32 [4], replicated, may hold values from 2 to 4096, as said below
- block_start: int32 [16], replicated, may hold values from 0 to 7680, as said below
Outputs:
- d_query: bfloat16 [8192, 16384], P('ctx', 'tp')
- update: float32 [2048, 16384], P('ctx', 'tp')
- new_moment: float32 [2048, 16384], P('ctx', 'tp')
- new_velocity: float32 [2048, 16384], P('ctx', 'tp')
The draws below stay inside these ranges and needn't reach their ends.
Inputs may be any that keep to these rules, and one draw needn't show every extreme that they name: `doc_lengths`: rounded up to multiples of 512, the lengths sum to 8192; the last block of every document holds 2 or more of its tokens. One document fills exactly 8 whole blocks. `block_start`: the starts are distinct multiples of 512 that together cover the packed sequence. The blocks are taken in aligned pairs (blocks 2i and 2i + 1): one of a pair starts at b and the other at 7680 - b.
All inputs are finite; a program needn't handle non-finite values.
Results may differ from the reference program's by a relative error of at most 0.008.
Values may be sent and summed in bfloat16 or wider, within the bound.
No kernel may reach another device: no remote copies, remote signals or barrier semaphores. Data moves between devices by JAX's collectives and lax.ppermute only.
A program may use at most 128 MiB of HBM per device.

```python
import math
import jax
import jax.numpy as jnp
from jax import lax

D = 16384
HEADS = 128
KV_HEADS = 8
HEAD_DIM = 128
BLOCK = 512
NDOCS = 4
SEQ = 8192
NBLK = 16
KV_UNITS = 1024


def draw_query(key, part):
    key = jax.random.fold_in(key, 21)
    sample = jax.random.truncated_normal(key, -4.0, 4.0, (SEQ, HEADS * HEAD_DIM), jnp.float32)
    return sample.astype(jnp.bfloat16)


def draw_keys(key, part):
    key = jax.random.fold_in(key, 23)
    sample = jax.random.truncated_normal(key, -4.0, 4.0, (SEQ, KV_UNITS), jnp.float32)
    return sample.astype(jnp.bfloat16)


def draw_inputs(key, part):
    key = jax.random.fold_in(key, 31)
    base_key, column_key, row_key = jax.random.split(key, 3)
    columns = jnp.exp(jax.random.uniform(column_key, (D,), jnp.float32, math.log(0.3), math.log(3.0)))
    column_ramp = 1.0 + 2.0 * jnp.arange(D, dtype=jnp.float32) / D
    row_scale = jnp.exp(jax.random.uniform(row_key, (SEQ, 1), jnp.float32, math.log(0.5), math.log(2.0)))
    sample = jax.random.truncated_normal(base_key, -4.0, 4.0, (SEQ, D), jnp.float32)
    return (sample * columns[None, :] * column_ramp[None, :] * row_scale).astype(jnp.bfloat16)


def draw_kv_weight(key, part):
    key = jax.random.fold_in(key, 51)
    base_key, column_key, row_key = jax.random.split(key, 3)
    columns = jnp.exp(jax.random.uniform(column_key, (D,), jnp.float32, 0.0, math.log(10.0)))
    column_ramp = 1.0 + 2.0 * jnp.arange(D, dtype=jnp.float32) / D
    row_scale = jnp.exp(jax.random.uniform(row_key, (2 * KV_UNITS, 1), jnp.float32, 0.0, math.log(10.0)))
    sample = jax.random.truncated_normal(base_key, -4.0, 4.0, (2 * KV_UNITS, D), jnp.float32)
    return sample * row_scale * columns[None, :] * column_ramp[None, :] / 30.0


def draw_moment(key, part):
    key = jax.random.fold_in(key, 61)
    base_key, column_key = jax.random.split(key, 2)
    columns = jnp.exp(jax.random.uniform(column_key, (D,), jnp.float32, 0.0, math.log(2.0)))
    column_ramp = 1.0 + 2.0 * jnp.arange(D, dtype=jnp.float32) / D
    sample = jax.random.truncated_normal(base_key, -4.0, 4.0, (2 * KV_UNITS, D), jnp.float32)
    return 10.0 * sample * columns[None, :] * column_ramp[None, :]


def draw_doc_lengths(key, part):
    key = jax.random.fold_in(key, 41)
    cut_key, fill_key, place_key = jax.random.split(key, 3)
    half_blocks = NBLK // 2
    rest_docs = NDOCS - 1
    cut_points = jnp.sort(jax.random.permutation(cut_key, half_blocks - 1)[:rest_docs - 1] + 1).astype(jnp.int32)
    bounds = jnp.concatenate([jnp.zeros((1,), jnp.int32), cut_points, jnp.full((1,), half_blocks, jnp.int32)])
    rest_counts = (bounds[1:] - bounds[:-1]).astype(jnp.int32)
    rest_fill = jax.random.randint(fill_key, (rest_docs,), 2, BLOCK + 1).astype(jnp.int32)
    rest_fill = jnp.where(jnp.arange(rest_docs) == 0, 2, rest_fill).astype(jnp.int32)
    rest_lengths = ((rest_counts - 1) * BLOCK + rest_fill).astype(jnp.int32)
    long_index = jax.random.randint(place_key, (), 0, NDOCS)
    positions = jnp.arange(NDOCS, dtype=jnp.int32)
    rest_pos = jnp.clip(positions - (positions > long_index).astype(jnp.int32), 0, rest_docs - 1)
    return jnp.where(positions == long_index, half_blocks * BLOCK, rest_lengths[rest_pos]).astype(jnp.int32)


def draw_block_start(key, part):
    key = jax.random.fold_in(key, 43)
    order_key, flip_key = jax.random.split(key)
    half_count = NBLK // 2
    shuffled = jax.random.permutation(order_key, half_count).astype(jnp.int32)
    flip_bits = jax.random.randint(flip_key, (half_count,), 0, 2)
    mirror = NBLK - 1 - shuffled
    leading = jnp.where(flip_bits == 1, mirror, shuffled)
    trailing = jnp.where(flip_bits == 1, shuffled, mirror)
    return (jnp.stack([leading, trailing], axis=1).reshape(NBLK) * BLOCK).astype(jnp.int32)


def shard_levels(key, shape, shards, smallest, largest):
    factor_of, own = 1.0, jax.random.fold_in(key, 6)
    for axis_at, blocks in shards:
        draws = jnp.exp(jax.random.uniform(jax.random.fold_in(own, axis_at), (blocks,), jnp.float32, smallest / len(shards), largest / len(shards)))
        factor_of = factor_of * jnp.repeat(draws, shape[axis_at] // blocks).reshape([-1 if axis == axis_at else 1 for axis in range(len(shape))])
    return factor_of


def centred(key, dims, scale, reach, cuts=(), kind=jnp.bfloat16):
    level = shard_levels(key, dims, cuts, -0.22, 0.18) if cuts else 1.0
    drawn = jax.random.normal(key, dims, jnp.float32) * scale * level
    return jnp.minimum(jnp.maximum(drawn, -reach), reach).astype(kind)


def setup_inputs(seed: int = 0) -> dict:
    key_list = jax.random.split(jax.random.key(seed), 11)
    query = draw_query(jax.random.fold_in(key_list[10], 71), 0)
    keys = draw_keys(jax.random.fold_in(key_list[10], 71), 0)
    values = centred(key_list[2], (SEQ, KV_HEADS * HEAD_DIM), 1.0, 6.0, ((0, 8),))
    d_out = centred(key_list[3], (SEQ, HEADS * HEAD_DIM), 1.0, 6.0, ((0, 8), (1, 16)))
    inputs = draw_inputs(jax.random.fold_in(key_list[10], 71), 0)
    kv_weight = draw_kv_weight(jax.random.fold_in(key_list[10], 71), 0)
    moment = draw_moment(jax.random.fold_in(key_list[10], 71), 0)
    velocity = jnp.clip(jnp.exp(math.log(30.0) - 4.6051701 * jax.random.uniform(key_list[7], (2 * KV_UNITS, D), jnp.float32) ** shard_levels(key_list[7], (2 * KV_UNITS, D), ((0, 8), (1, 16)), -0.2, 0.2)), 0.3, 30.0)
    doc_lengths = draw_doc_lengths(jax.random.fold_in(key_list[10], 71), 0)
    block_start = draw_block_start(jax.random.fold_in(key_list[10], 71), 0)
    return {"query": query, "keys": keys, "values": values, "d_out": d_out, "inputs": inputs, "kv_weight": kv_weight, "moment": moment, "velocity": velocity, "doc_lengths": doc_lengths, "block_start": block_start}


beta_one = 0.9
beta_two = 0.999
first_correction = 1.0 - 0.9 ** 10
second_correction = 1.0 - 0.999 ** 10
adam_eps = 1e-06
norm_eps = 1e-06

def layout(block_start, doc_lengths, seq_len):
    offsets = jnp.arange(seq_len, dtype=jnp.int32) % BLOCK
    places = (jnp.repeat(block_start, BLOCK, total_repeat_length=seq_len) + offsets).astype(jnp.int32)
    padded = ((doc_lengths + BLOCK - 1) // BLOCK * BLOCK).astype(jnp.int32)
    doc_ends = jnp.cumsum(padded).astype(jnp.int32)
    doc_starts = (doc_ends - padded).astype(jnp.int32)
    doc_owner = lax.optimization_barrier(jnp.sum((places[:, None] >= doc_ends[None, :]).astype(jnp.int32), axis=1)).astype(jnp.int32)
    doc_picks = doc_owner[:, None] == jnp.arange(doc_lengths.shape[0], dtype=jnp.int32)[None, :]
    limits = lax.optimization_barrier(jnp.sum(jnp.where(doc_picks, (doc_starts + doc_lengths)[None, :], 0), axis=1)).astype(jnp.int32)
    return (places, doc_owner, places < limits)

def reference(query, keys, values, d_out, inputs, kv_weight, moment, velocity, doc_lengths, block_start):
    places, doc_owner, doc_valid = layout(block_start, doc_lengths, SEQ)
    allowed = (doc_owner[:, None] == doc_owner[None, :]) & (places[None, :] <= places[:, None]) & doc_valid[None, :]
    masked_out = jnp.where(doc_valid[:, None], d_out, jnp.zeros_like(d_out))
    scaling = HEAD_DIM ** (-0.5)
    group_size = HEADS // KV_HEADS
    highest = lax.Precision.HIGHEST

    def one_head(head_index):
        shared_head = head_index // group_size
        query_head = lax.dynamic_slice_in_dim(query, head_index * HEAD_DIM, HEAD_DIM, 1).astype(jnp.float32)
        out_head = lax.dynamic_slice_in_dim(masked_out, head_index * HEAD_DIM, HEAD_DIM, 1).astype(jnp.float32)
        key_head = lax.dynamic_slice_in_dim(keys, shared_head * HEAD_DIM, HEAD_DIM, 1).astype(jnp.float32)
        value_head = lax.dynamic_slice_in_dim(values, shared_head * HEAD_DIM, HEAD_DIM, 1).astype(jnp.float32)
        scores = jnp.dot(query_head, key_head.T, precision=highest, preferred_element_type=jnp.float32) * scaling
        scores = jnp.where(allowed, scores, -jnp.inf)
        probabilities = jax.nn.softmax(scores, axis=-1)
        slopes = jnp.dot(out_head, value_head.T, precision=highest, preferred_element_type=jnp.float32)
        delta_rows = lax.optimization_barrier(jnp.sum(probabilities * slopes, axis=-1))
        dscore = probabilities * (slopes - delta_rows[:, None])
        prob_low = lax.optimization_barrier(probabilities.astype(jnp.bfloat16)).astype(jnp.float32)
        dscore_low = lax.optimization_barrier(dscore.astype(jnp.bfloat16)).astype(jnp.float32)
        grad_query = jnp.dot(dscore_low, key_head, precision=highest, preferred_element_type=jnp.float32) * scaling
        grad_key = jnp.dot(dscore_low.T, query_head, precision=highest, preferred_element_type=jnp.float32) * scaling
        grad_value = jnp.dot(prob_low.T, out_head, precision=highest, preferred_element_type=jnp.float32)
        return (grad_query.astype(jnp.bfloat16), grad_key, grad_value)
    query_grads, key_grads, value_grads = lax.map(one_head, jnp.arange(HEADS, dtype=jnp.int32))
    d_query = jnp.transpose(query_grads, (1, 0, 2)).reshape(SEQ, HEADS * HEAD_DIM)
    key_sum = lax.optimization_barrier(jnp.sum(key_grads.reshape(KV_HEADS, group_size, SEQ, HEAD_DIM), axis=1))
    value_sum = lax.optimization_barrier(jnp.sum(value_grads.reshape(KV_HEADS, group_size, SEQ, HEAD_DIM), axis=1))
    grad_keys = jnp.transpose(key_sum, (1, 0, 2)).reshape(SEQ, KV_HEADS * HEAD_DIM)
    grad_values = jnp.transpose(value_sum, (1, 0, 2)).reshape(SEQ, KV_HEADS * HEAD_DIM)
    both_grads = jnp.concatenate([grad_keys, grad_values], axis=1)
    weight_grad = jnp.dot(both_grads.T, inputs.astype(jnp.float32), precision=highest, preferred_element_type=jnp.float32)
    new_moment = beta_one * moment + (1.0 - beta_one) * weight_grad
    new_velocity = beta_two * velocity + (1.0 - beta_two) * weight_grad * weight_grad
    direction = new_moment / first_correction / (jnp.sqrt(new_velocity / second_correction) + adam_eps)
    trust_ratio = jnp.sqrt(lax.optimization_barrier(jnp.sum(kv_weight * kv_weight, axis=1))) / jnp.sqrt(lax.optimization_barrier(jnp.sum(direction * direction, axis=1)) + norm_eps)
    update = trust_ratio[:, None] * direction
    return (d_query, update, new_moment, new_velocity)
```

```python
import functools

import jax
import jax.numpy as jnp
from jax import lax
from jax.experimental import pallas as pl
from jax.experimental.pallas import tpu as pltpu
from jax.sharding import PartitionSpec as P

KV_HEADS = 8
HEAD_DIM = 128
BLOCK = 512
NBLK = 16
NDOCS = 4
DOC_BLOCKS = 8
TOK = 1024
ROWS = 256
CHUNK = 256
HEADS_IN = 4
LANES = HEADS_IN * ROWS
SCALE = HEAD_DIM**-0.5
EXP_SCALE = SCALE * 1.4426950408889634
LOW = -1e30
CORES = 2
RING = 4
SIDE = 4

beta_one = 0.9
beta_two = 0.999
first_correction = 1.0 - 0.9**10
second_correction = 1.0 - 0.999**10
adam_eps = 1e-06
norm_eps = 1e-06


def product(a, b):
    return lax.dot_general(a, b, (((1,), (0,)), ((), ())), preferred_element_type=jnp.float32)


def product_nt(a, b):
    return lax.dot_general(a, b, (((1,), (1,)), ((), ())), preferred_element_type=jnp.float32)


def attention_kernel(doc_ref, start_ref, ctx_ref, *refs):
    query_refs, grad_refs, refs = refs[0:2], refs[2:4], refs[4:]
    kv_pieces, refs = refs[:8], refs[8:]
    dq_refs, refs = refs[:2], refs[2:]
    totals, refs = refs[:2], refs[2:]
    kv_ref, dk_ref, dv_ref, q_rows, o_rows, e_ref, dp_ref, top_ref, inv_ref = refs[:9]
    own_query, own_grad, arrivals = refs[9:]
    per_block = BLOCK // CHUNK
    me = ctx_ref[0]
    my_z, my_core = me // CORES, me % CORES
    wide = HEADS_IN * HEAD_DIM
    own = pl.ds(pl.multiple_of(my_core * wide, wide), wide)
    moves = [
        (kv_pieces[i], kv_ref.at[pl.ds(i * TOK, TOK), :]) for i in range(CORES * RING)
    ] + [(query_refs[0].at[:, own], own_query), (grad_refs[0].at[:, own], own_grad)]
    copies = [
        pltpu.make_async_copy(source, target, arrivals.at[i])
        for i, (source, target) in enumerate(moves)
    ]
    for copy in copies:
        copy.start()
    dk_ref[...] = jnp.zeros_like(dk_ref)
    dv_ref[...] = jnp.zeros_like(dv_ref)
    for b in range(NBLK):
        ctx = b // 2
        away = lax.rem(ctx // CORES - my_z + RING, RING)
        other = jnp.where(ctx % CORES == my_core, 0, 1)
        inv_ref[start_ref[b] // BLOCK] = (other * RING + away) * 2 + b % 2

    for copy in copies:
        copy.wait()
    query_refs, grad_refs = (own_query, query_refs[1]), (own_grad, grad_refs[1])

    def tile_step(source, dq_ref, blk, sub):
        ctx = me if source == 0 else my_z * CORES + (1 - my_core)
        tile = blk * (BLOCK // ROWS) + sub
        pos = start_ref[ctx * 2 + blk] // BLOCK
        begin = jnp.int32(0)
        first = jnp.int32(0)
        limit = jnp.int32(0)
        for d in range(NDOCS):
            length = doc_ref[d]
            size = (length + BLOCK - 1) // BLOCK
            inside = (pos >= begin) & (pos < begin + size)
            first = jnp.where(inside, begin, first)
            limit = jnp.where(inside, begin * BLOCK + length, limit)
            begin = begin + size
        real = limit - (pos * BLOCK + sub * ROWS)
        n_before = pos - first
        out_rows = pl.ds(pl.multiple_of(tile * ROWS, ROWS), ROWS)

        @pl.when(real <= 0)
        def _():
            dq_ref[out_rows, :] = jnp.zeros((ROWS, HEADS_IN * HEAD_DIM), jnp.bfloat16)

        @pl.when(real > 0)
        def _():
            live = lax.broadcasted_iota(jnp.int32, (ROWS, HEAD_DIM), 0) < real
            for i in range(HEADS_IN):
                cols = slice(i * HEAD_DIM, (i + 1) * HEAD_DIM)
                part = slice(i * ROWS, (i + 1) * ROWS)
                q_head = query_refs[source][out_rows, cols]
                o_head = grad_refs[source][out_rows, cols]
                o_head = jnp.where(live, o_head, jnp.zeros((), jnp.bfloat16))
                q_rows[part, :] = q_head
                o_rows[part, :] = o_head

            def phase_one(chunk, j, size, state, masked):
                top, total, weighted = state
                at = pl.ds(pl.multiple_of(chunk * CHUNK, CHUNK), size)
                keep = pl.ds(pl.multiple_of(j * CHUNK, CHUNK), size)
                scores = product_nt(kv_ref[at, :HEAD_DIM], q_rows[...])
                slopes = product_nt(kv_ref[at, HEAD_DIM:], o_rows[...])
                if masked:
                    key_row = lax.broadcasted_iota(jnp.int32, (size, LANES), 0)
                    query_row = lax.broadcasted_iota(jnp.int32, (size, LANES), 1) % ROWS
                    scores = jnp.where(key_row <= query_row + sub * ROWS, scores, LOW)
                new_top = jnp.maximum(top, jnp.max(scores, axis=0, keepdims=True) * EXP_SCALE)
                weights = jnp.exp2(scores * EXP_SCALE - new_top)
                shrink = jnp.exp2(top - new_top)
                total = total * shrink + jnp.sum(weights, axis=0, keepdims=True)
                weighted = weighted * shrink + jnp.sum(weights * slopes, axis=0, keepdims=True)
                e_ref[keep, :] = weights.astype(jnp.bfloat16)
                dp_ref[keep, :] = slopes
                top_ref[j] = jnp.broadcast_to(new_top, (8, LANES))
                return new_top, total, weighted

            def phase_two(chunk, j, size, stats, acc):
                top, inverse, delta = stats
                at = pl.ds(pl.multiple_of(chunk * CHUNK, CHUNK), size)
                keep = pl.ds(pl.multiple_of(j * CHUNK, CHUNK), size)
                factor = jnp.exp2(top_ref[j, 0:1, :] - top) * inverse
                probs = e_ref[keep, :].astype(jnp.float32) * factor
                dscore = (probs * (dp_ref[keep, :] - delta)).astype(jnp.bfloat16)
                dv_ref[at, :] += product(probs.astype(jnp.bfloat16), o_rows[...])
                dk_ref[at, :] += product(dscore, q_rows[...])
                return acc + lax.dot_general(kv_ref[at, :HEAD_DIM], dscore, (((0,), (0,)), ((), ())), preferred_element_type=jnp.float32)

            def sweep(visit, state):
                def whole(j, state):
                    return visit(inv_ref[first + j] * per_block, j * per_block, BLOCK, state, False)

                state = lax.fori_loop(0, n_before, whole, state)
                return visit(inv_ref[pos] * per_block, n_before * per_block, (sub + 1) * ROWS, state, True)

            none_yet = (
                jnp.full((1, LANES), LOW, jnp.float32),
                jnp.zeros((1, LANES), jnp.float32),
                jnp.zeros((1, LANES), jnp.float32),
            )
            top, total, weighted = sweep(phase_one, none_yet)
            inverse = 1.0 / total
            stats = (top, inverse, weighted * inverse)
            no_grad = jnp.zeros((HEAD_DIM, LANES), jnp.float32)
            acc = sweep(
                lambda chunk, j, size, acc, masked: phase_two(chunk, j, size, stats, acc), no_grad
            )
            out = (acc * SCALE).T.astype(jnp.bfloat16)
            for i in range(HEADS_IN):
                cols = slice(i * HEAD_DIM, (i + 1) * HEAD_DIM)
                dq_ref[out_rows, cols] = out[i * ROWS : (i + 1) * ROWS, :]

    for source in range(CORES):

        def step(blk, _, source=source):
            for sub in range(BLOCK // ROWS):
                tile_step(source, dq_refs[source], blk, sub)
            return 0

        lax.fori_loop(0, TOK // BLOCK, step, 0)
    for i in range(8):
        rows = slice(i * TOK, (i + 1) * TOK)
        out = slice((i % RING) * TOK, (i % RING + 1) * TOK)
        totals[i // RING][out, :HEAD_DIM] = (dk_ref[rows, :] * SCALE).astype(jnp.bfloat16)
        totals[i // RING][out, HEAD_DIM:] = dv_ref[rows, :].astype(jnp.bfloat16)


def attention(doc_lengths, block_start, ctx, queries, out_grads, kv_pieces):
    n_keys = DOC_BLOCKS * BLOCK
    here = pl.BlockSpec(memory_space=pl.ANY)
    smem = pl.BlockSpec(memory_space=pltpu.SMEM)
    vmem = pl.BlockSpec(memory_space=pltpu.VMEM)
    piece = jax.ShapeDtypeStruct((RING * TOK, 2 * HEAD_DIM), jnp.bfloat16)
    half = jax.ShapeDtypeStruct((TOK, HEADS_IN * HEAD_DIM), jnp.bfloat16)
    return pl.pallas_call(
        attention_kernel,
        out_shape=(half, half, piece, piece),
        in_specs=[smem] * 3 + [here, vmem, here, vmem] + [here] * 8,
        out_specs=(vmem,) * 4,
        scratch_shapes=[
            pltpu.VMEM((NBLK * BLOCK, 2 * HEAD_DIM), jnp.bfloat16),
            pltpu.VMEM((NBLK * BLOCK, HEAD_DIM), jnp.float32),
            pltpu.VMEM((NBLK * BLOCK, HEAD_DIM), jnp.float32),
            pltpu.VMEM((LANES, HEAD_DIM), jnp.bfloat16),
            pltpu.VMEM((LANES, HEAD_DIM), jnp.bfloat16),
            pltpu.VMEM((n_keys, LANES), jnp.bfloat16),
            pltpu.VMEM((n_keys, LANES), jnp.float32),
            pltpu.VMEM((n_keys // CHUNK, 8, LANES), jnp.float32),
            pltpu.SMEM((NBLK,), jnp.int32),
            pltpu.VMEM((TOK, HEADS_IN * HEAD_DIM), jnp.bfloat16),
            pltpu.VMEM((TOK, HEADS_IN * HEAD_DIM), jnp.bfloat16),
            pltpu.SemaphoreType.DMA((CORES * RING + 2,)),
        ],
        compiler_params=pltpu.CompilerParams(vmem_limit_bytes=60 * 2**20),
        name="attention_backward",
    )(doc_lengths, block_start, ctx, *queries, *out_grads, *kv_pieces)


def weight_kernel(other, at_ref, *refs):
    lines, x_ref, out_ref, turned = refs[: 2 * SIDE], *refs[2 * SIDE :]
    my_z, my_core, my_y, my_x = at_ref[0], at_ref[1], at_ref[2], at_ref[3]
    part_rows = TOK // 4
    for order in range(2):
        for outer in range(SIDE):
            for inner in range(SIDE):
                down, along = (inner, outer) if order == 0 else (outer, inner)
                y, x = lax.rem(my_y + down, SIDE), lax.rem(my_x + along, SIDE)
                part = lines[order * SIDE + outer][inner].T
                turned[lax.rem(x, 2) * 2 + order, y * 2 + x // 2] = part
    for away in range(RING):
        core = my_core if other == 0 else 1 - my_core
        owner = lax.rem(my_z + away, RING) * CORES + core
        units = pl.ds(pl.multiple_of(owner // 4 * HEAD_DIM, HEAD_DIM), HEAD_DIM)
        head = lax.rem(owner, 4) * 2
        total = jnp.zeros((2 * HEAD_DIM, x_ref.shape[1]), jnp.float32)
        for i in range(4):
            left = jnp.concatenate([turned[i, head, units, :], turned[i, head + 1, units, :]], axis=0)
            total = total + product(left, x_ref[i * part_rows : (i + 1) * part_rows, :])
        out_ref[away] = total.astype(jnp.bfloat16)


def weight_products(other, place, lines, inputs):
    features = inputs.shape[1]
    smem = pl.BlockSpec(memory_space=pltpu.SMEM)
    vmem = pl.BlockSpec(memory_space=pltpu.VMEM)
    return pl.pallas_call(
        functools.partial(weight_kernel, other),
        out_shape=jax.ShapeDtypeStruct((RING, 2 * HEAD_DIM, features), jnp.bfloat16),
        in_specs=[smem] + [vmem] * (2 * SIDE + 1),
        out_specs=vmem,
        scratch_shapes=[pltpu.VMEM((4, KV_HEADS, 2 * HEAD_DIM, TOK // 4), jnp.bfloat16)],
        compiler_params=pltpu.CompilerParams(vmem_limit_bytes=32 * 2**20),
        name="weight_products",
    )(place, *lines, inputs)


def other_core(x):
    return lax.ppermute(x, "ctx", [(i, i ^ 1) for i in range(CORES * RING)])


def from_z(x, away):
    return lax.ppermute(
        x, "ctx", [(((i // CORES + away) % RING) * CORES + i % CORES, i) for i in range(CORES * RING)]
    )


def other_of_pair(x):
    return lax.ppermute(x, "tp", [(i, i ^ 1) for i in range(SIDE * SIDE)])


def from_y(x, away):
    return lax.ppermute(
        x, "tp", [(((i // SIDE + away) % SIDE) * SIDE + i % SIDE, i) for i in range(SIDE * SIDE)]
    )


def from_x(x, away):
    return lax.ppermute(
        x, "tp", [(i // SIDE * SIDE + (i % SIDE + away) % SIDE, i) for i in range(SIDE * SIDE)]
    )


def gathered(x, hop):
    return [x] + [hop(x, away) for away in range(1, SIDE)]


def around(arrays):
    near = [(hop(x, 1), hop(x, SIDE - 1)) for x, hop in arrays]
    near = lax.optimization_barrier(near)
    far = []
    for (x, hop), (after, before) in zip(arrays, near):
        half = x.shape[0] // 2
        far.append((hop(after[:half], 1), hop(before[half:], SIDE - 1)))
    far = lax.optimization_barrier(far)
    return [
        [x, after, jnp.concatenate(across, axis=0), before]
        for (x, hop), (after, before), across in zip(arrays, near, far)
    ]


def summed(x, hop):
    total = x
    for away in range(1, SIDE):
        total = total + hop(x, away)
    return total


def reduce_ctx(keep, arrived, rows):
    bf16, f32 = jnp.bfloat16, jnp.float32
    half = rows // 2

    def pair(away, low, high):
        at = slice(away * rows + low, away * rows + high)
        return keep[at].astype(f32) + arrived[at].astype(f32)

    ahead, behind = lax.optimization_barrier(
        (pair(2, 0, half).astype(bf16), pair(2, half, rows).astype(bf16))
    )
    from_before, from_after = lax.optimization_barrier(
        (from_z(ahead, RING - 1), from_z(behind, 1))
    )
    up = jnp.concatenate([pair(1, 0, half) + from_before.astype(f32), pair(1, half, rows)], axis=0)
    down = jnp.concatenate([pair(3, 0, half), pair(3, half, rows) + from_after.astype(f32)], axis=0)
    up, down = lax.optimization_barrier((up.astype(bf16), down.astype(bf16)))
    arrived_up, arrived_down = lax.optimization_barrier((from_z(up, RING - 1), from_z(down, 1)))
    return pair(0, 0, rows) + arrived_up.astype(f32) + arrived_down.astype(f32)


def shards(
    query, keys, values, d_out, inputs, kv_weight, moment, velocity, doc_lengths, block_start
):
    ctx, tp = lax.axis_index("ctx"), lax.axis_index("tp")
    my_z, my_core = ctx // CORES, ctx % CORES
    head_at = (tp // 2) * HEAD_DIM
    wide = HEADS_IN * HEAD_DIM
    bf16, f32 = jnp.bfloat16, jnp.float32
    own_kv = jnp.concatenate(
        [
            lax.dynamic_slice_in_dim(keys, head_at, HEAD_DIM, 1),
            lax.dynamic_slice_in_dim(values, head_at, HEAD_DIM, 1),
        ],
        axis=1,
    )
    same_core = around([(own_kv, from_z)])[0]
    cross_core = [other_core(piece) for piece in same_core]

    def for_other_core(x):
        return other_core(lax.dynamic_slice_in_dim(x, (1 - my_core) * wide, wide, 1))

    dq_own, dq_other, keep, send = attention(
        doc_lengths,
        block_start,
        ctx.reshape(1),
        (query, for_other_core(query)),
        (d_out, for_other_core(d_out)),
        same_core + cross_core,
    )
    place = jnp.stack([my_z, my_core, tp // SIDE, tp % SIDE]).astype(jnp.int32)
    even = tp % 2 == 0
    gradient = reduce_ctx(keep, other_core(send), TOK)
    dq_back = other_core(dq_other)
    d_query = jnp.where(
        my_core == 0,
        jnp.concatenate([dq_own, dq_back], axis=1),
        jnp.concatenate([dq_back, dq_own], axis=1),
    )
    gradient, d_query = lax.optimization_barrier((gradient, d_query))
    upper, lower = gradient[: TOK // 2], gradient[TOK // 2 :]
    given = jnp.where(even, lower, upper).astype(bf16)
    kept = jnp.where(even, upper, lower)
    own_part = (kept + other_of_pair(given).astype(f32)).astype(bf16)
    quarter = TOK // 4
    line_y = jnp.stack(gathered(own_part[:quarter], from_y))
    line_x = jnp.stack(gathered(own_part[quarter:], from_x))
    line_y, line_x = lax.optimization_barrier((line_y, line_x))
    far_x, far_y, *near = lax.optimization_barrier(
        [from_x(line_y, 2), from_y(line_x, 2)]
        + [hop(line, away) for away in (1, 3) for line, hop in ((line_y, from_x), (line_x, from_y))]
    )
    along_x = [line_y, near[0], far_x, near[2]]
    along_y = [line_x, near[1], far_y, near[3]]
    features = inputs.shape[1]
    flat = (RING * 2 * HEAD_DIM, features)
    for_other = weight_products(1, place, along_x + along_y, inputs).reshape(flat)
    arrived = other_core(for_other)
    for_mine = weight_products(0, place, along_x + along_y, inputs).reshape(flat)
    weight_grad = reduce_ctx(for_mine, arrived, 2 * HEAD_DIM)
    new_moment = beta_one * moment + (1.0 - beta_one) * weight_grad
    new_velocity = beta_two * velocity + (1.0 - beta_two) * weight_grad * weight_grad
    direction = (
        new_moment / first_correction / (jnp.sqrt(new_velocity / second_correction) + adam_eps)
    )
    squares = jnp.stack(
        [jnp.sum(kv_weight * kv_weight, axis=1), jnp.sum(direction * direction, axis=1)]
    )
    weight_square, update_square = summed(summed(squares, from_y), from_x)
    trust_ratio = jnp.sqrt(weight_square) / jnp.sqrt(update_square + norm_eps)
    update = trust_ratio[:, None] * direction
    return (d_query, update, new_moment, new_velocity)


def solution(mesh):
    split = P("ctx", "tp")
    rows = P("ctx", None)
    return jax.shard_map(
        shards,
        mesh=mesh,
        in_specs=(split, rows, rows, split, split, split, split, split, P(), P()),
        out_specs=(split,) * 4,
        check_vma=False,
    )
```

```python
import functools

import jax
import jax.numpy as jnp
from jax import lax
from jax.experimental import pallas as pl
from jax.experimental.pallas import tpu as pltpu
from jax.sharding import PartitionSpec as P

KV_HEADS = 8
HEAD_DIM = 128
BLOCK = 512
NBLK = 16
NDOCS = 4
DOC_BLOCKS = 8
TOK = 1024
ROWS = 256
CHUNK = 256
HEADS_IN = 4
LANES = HEADS_IN * ROWS
SCALE = HEAD_DIM**-0.5
EXP_SCALE = SCALE * 1.4426950408889634
LOW = -1e30
CORES = 2
RING = 4
SIDE = 4

beta_one = 0.9
beta_two = 0.999
first_correction = 1.0 - 0.9**10
second_correction = 1.0 - 0.999**10
adam_eps = 1e-06
norm_eps = 1e-06


def product(a, b):
    return lax.dot_general(a, b, (((1,), (0,)), ((), ())), preferred_element_type=jnp.float32)


def product_nt(a, b):
    return lax.dot_general(a, b, (((1,), (1,)), ((), ())), preferred_element_type=jnp.float32)


def attention_kernel(doc_ref, start_ref, ctx_ref, *refs):
    query_refs, grad_refs, refs = refs[0:2], refs[2:4], refs[4:]
    kv_pieces, refs = refs[:8], refs[8:]
    dq_refs, refs = refs[:2], refs[2:]
    totals, refs = refs[:2], refs[2:]
    kv_ref, dk_ref, dv_ref, q_rows, o_rows, e_ref, dp_ref, top_ref, inv_ref = refs[:9]
    own_query, own_grad, other_query, other_grad, arrivals = refs[9:]
    per_block = BLOCK // CHUNK
    me = ctx_ref[0]
    my_z, my_core = me // CORES, me % CORES
    wide = HEADS_IN * HEAD_DIM
    own = pl.ds(pl.multiple_of(my_core * wide, wide), wide)
    moves = [
        (kv_pieces[i], kv_ref.at[pl.ds(i * TOK, TOK), :]) for i in range(CORES * RING)
    ] + [
        (query_refs[0].at[:, own], own_query),
        (grad_refs[0].at[:, own], own_grad),
        (query_refs[1], other_query),
        (grad_refs[1], other_grad),
    ]
    copies = [
        pltpu.make_async_copy(source, target, arrivals.at[i])
        for i, (source, target) in enumerate(moves)
    ]
    for copy in copies:
        copy.start()
    dk_ref[...] = jnp.zeros_like(dk_ref)
    dv_ref[...] = jnp.zeros_like(dv_ref)
    for b in range(NBLK):
        ctx = b // 2
        away = lax.rem(ctx // CORES - my_z + RING, RING)
        other = jnp.where(ctx % CORES == my_core, 0, 1)
        inv_ref[start_ref[b] // BLOCK] = (other * RING + away) * 2 + b % 2

    for copy in copies:
        copy.wait()
    query_refs, grad_refs = (own_query, other_query), (own_grad, other_grad)

    def tile_step(source, dq_ref, blk, sub):
        ctx = me if source == 0 else my_z * CORES + (1 - my_core)
        tile = blk * (BLOCK // ROWS) + sub
        pos = start_ref[ctx * 2 + blk] // BLOCK
        begin = jnp.int32(0)
        first = jnp.int32(0)
        limit = jnp.int32(0)
        for d in range(NDOCS):
            length = doc_ref[d]
            size = (length + BLOCK - 1) // BLOCK
            inside = (pos >= begin) & (pos < begin + size)
            first = jnp.where(inside, begin, first)
            limit = jnp.where(inside, begin * BLOCK + length, limit)
            begin = begin + size
        real = limit - (pos * BLOCK + sub * ROWS)
        n_before = pos - first
        out_rows = pl.ds(pl.multiple_of(tile * ROWS, ROWS), ROWS)

        @pl.when(real <= 0)
        def _():
            dq_ref[out_rows, :] = jnp.zeros((ROWS, HEADS_IN * HEAD_DIM), jnp.bfloat16)

        @pl.when(real > 0)
        def _():
            live = lax.broadcasted_iota(jnp.int32, (ROWS, HEAD_DIM), 0) < real
            for i in range(HEADS_IN):
                cols = slice(i * HEAD_DIM, (i + 1) * HEAD_DIM)
                part = slice(i * ROWS, (i + 1) * ROWS)
                q_head = query_refs[source][out_rows, cols]
                o_head = grad_refs[source][out_rows, cols]
                o_head = jnp.where(live, o_head, jnp.zeros((), jnp.bfloat16))
                q_rows[part, :] = q_head
                o_rows[part, :] = o_head

            def phase_one(chunk, j, size, state, masked):
                top, total, weighted = state
                at = pl.ds(pl.multiple_of(chunk * CHUNK, CHUNK), size)
                keep = pl.ds(pl.multiple_of(j * CHUNK, CHUNK), size)
                scores = product_nt(kv_ref[at, :HEAD_DIM], q_rows[...])
                slopes = product_nt(kv_ref[at, HEAD_DIM:], o_rows[...])
                if masked:
                    key_row = lax.broadcasted_iota(jnp.int32, (size, LANES), 0)
                    query_row = lax.broadcasted_iota(jnp.int32, (size, LANES), 1) % ROWS
                    scores = jnp.where(key_row <= query_row + sub * ROWS, scores, LOW)
                new_top = jnp.maximum(top, jnp.max(scores, axis=0, keepdims=True) * EXP_SCALE)
                weights = jnp.exp2(scores * EXP_SCALE - new_top)
                shrink = jnp.exp2(top - new_top)
                total = total * shrink + jnp.sum(weights, axis=0, keepdims=True)
                weighted = weighted * shrink + jnp.sum(weights * slopes, axis=0, keepdims=True)
                e_ref[keep, :] = weights.astype(jnp.bfloat16)
                dp_ref[keep, :] = slopes
                top_ref[j] = jnp.broadcast_to(new_top, (8, LANES))
                return new_top, total, weighted

            def phase_two(chunk, j, size, stats, acc):
                top, inverse, delta = stats
                at = pl.ds(pl.multiple_of(chunk * CHUNK, CHUNK), size)
                keep = pl.ds(pl.multiple_of(j * CHUNK, CHUNK), size)
                factor = jnp.exp2(top_ref[j, 0:1, :] - top) * inverse
                probs = e_ref[keep, :].astype(jnp.float32) * factor
                dscore = (probs * (dp_ref[keep, :] - delta)).astype(jnp.bfloat16)
                dv_ref[at, :] += product(probs.astype(jnp.bfloat16), o_rows[...])
                dk_ref[at, :] += product(dscore, q_rows[...])
                return acc + lax.dot_general(kv_ref[at, :HEAD_DIM], dscore, (((0,), (0,)), ((), ())), preferred_element_type=jnp.float32)

            def sweep(visit, state):
                def whole(j, state):
                    return visit(inv_ref[first + j] * per_block, j * per_block, BLOCK, state, False)

                state = lax.fori_loop(0, n_before, whole, state)
                return visit(inv_ref[pos] * per_block, n_before * per_block, (sub + 1) * ROWS, state, True)

            none_yet = (
                jnp.full((1, LANES), LOW, jnp.float32),
                jnp.zeros((1, LANES), jnp.float32),
                jnp.zeros((1, LANES), jnp.float32),
            )
            top, total, weighted = sweep(phase_one, none_yet)
            inverse = 1.0 / total
            stats = (top, inverse, weighted * inverse)
            no_grad = jnp.zeros((HEAD_DIM, LANES), jnp.float32)
            acc = sweep(
                lambda chunk, j, size, acc, masked: phase_two(chunk, j, size, stats, acc), no_grad
            )
            out = (acc * SCALE).T.astype(jnp.bfloat16)
            for i in range(HEADS_IN):
                cols = slice(i * HEAD_DIM, (i + 1) * HEAD_DIM)
                dq_ref[out_rows, cols] = out[i * ROWS : (i + 1) * ROWS, :]

    for source in range(CORES):

        def step(blk, _, source=source):
            for sub in range(BLOCK // ROWS):
                tile_step(source, dq_refs[source], blk, sub)
            return 0

        lax.fori_loop(0, TOK // BLOCK, step, 0)
    for i in range(8):
        rows = slice(i * TOK, (i + 1) * TOK)
        out = slice((i % RING) * TOK, (i % RING + 1) * TOK)
        totals[i // RING][out, :HEAD_DIM] = (dk_ref[rows, :] * SCALE).astype(jnp.bfloat16)
        totals[i // RING][out, HEAD_DIM:] = dv_ref[rows, :].astype(jnp.bfloat16)


def attention(doc_lengths, block_start, ctx, queries, out_grads, kv_pieces):
    n_keys = DOC_BLOCKS * BLOCK
    here = pl.BlockSpec(memory_space=pl.ANY)
    smem = pl.BlockSpec(memory_space=pltpu.SMEM)
    vmem = pl.BlockSpec(memory_space=pltpu.VMEM)
    piece = jax.ShapeDtypeStruct((RING * TOK, 2 * HEAD_DIM), jnp.bfloat16)
    half = jax.ShapeDtypeStruct((TOK, HEADS_IN * HEAD_DIM), jnp.bfloat16)
    return pl.pallas_call(
        attention_kernel,
        out_shape=(half, half, piece, piece),
        in_specs=[smem] * 3 + [here] * 12,
        out_specs=(vmem,) * 4,
        scratch_shapes=[
            pltpu.VMEM((NBLK * BLOCK, 2 * HEAD_DIM), jnp.bfloat16),
            pltpu.VMEM((NBLK * BLOCK, HEAD_DIM), jnp.float32),
            pltpu.VMEM((NBLK * BLOCK, HEAD_DIM), jnp.float32),
            pltpu.VMEM((LANES, HEAD_DIM), jnp.bfloat16),
            pltpu.VMEM((LANES, HEAD_DIM), jnp.bfloat16),
            pltpu.VMEM((n_keys, LANES), jnp.bfloat16),
            pltpu.VMEM((n_keys, LANES), jnp.float32),
            pltpu.VMEM((n_keys // CHUNK, 8, LANES), jnp.float32),
            pltpu.SMEM((NBLK,), jnp.int32),
        ]
        + [pltpu.VMEM((TOK, HEADS_IN * HEAD_DIM), jnp.bfloat16)] * 4
        + [pltpu.SemaphoreType.DMA((CORES * RING + 4,))],
        compiler_params=pltpu.CompilerParams(vmem_limit_bytes=60 * 2**20),
        name="attention_backward",
    )(doc_lengths, block_start, ctx, *queries, *out_grads, *kv_pieces)


def weight_kernel(other, at_ref, *refs):
    lines, inputs_ref, out_ref, turned, x_ref, arrival = refs[: 2 * SIDE], *refs[2 * SIDE :]
    copy = pltpu.make_async_copy(inputs_ref, x_ref, arrival)
    copy.start()
    my_z, my_core, my_y, my_x = at_ref[0], at_ref[1], at_ref[2], at_ref[3]
    part_rows = TOK // 4
    core = my_core if other == 0 else 1 - my_core
    for order in range(2):
        for outer in range(SIDE):
            for inner in range(SIDE):
                down, along = (inner, outer) if order == 0 else (outer, inner)
                y, x = lax.rem(my_y + down, SIDE), lax.rem(my_x + along, SIDE)

                @pl.when(lax.rem(y, CORES) == core)
                def _(part=lines[order * SIDE + outer], inner=inner, order=order, y=y, x=x):
                    turned[lax.rem(x, 2) * 2 + order, y * 2 + x // 2] = part[inner].T

    copy.wait()
    for away in range(RING):
        owner = lax.rem(my_z + away, RING) * CORES + core
        units = pl.ds(pl.multiple_of(owner // 4 * HEAD_DIM, HEAD_DIM), HEAD_DIM)
        head = lax.rem(owner, 4) * 2
        total = jnp.zeros((2 * HEAD_DIM, x_ref.shape[1]), jnp.float32)
        for i in range(4):
            left = jnp.concatenate([turned[i, head, units, :], turned[i, head + 1, units, :]], axis=0)
            total = total + product(left, x_ref[i * part_rows : (i + 1) * part_rows, :])
        out_ref[away] = total.astype(jnp.bfloat16)


def weight_products(other, place, lines, inputs):
    features = inputs.shape[1]
    smem = pl.BlockSpec(memory_space=pltpu.SMEM)
    vmem = pl.BlockSpec(memory_space=pltpu.VMEM)
    return pl.pallas_call(
        functools.partial(weight_kernel, other),
        out_shape=jax.ShapeDtypeStruct((RING, 2 * HEAD_DIM, features), jnp.bfloat16),
        in_specs=[smem] + [vmem] * (2 * SIDE) + [pl.BlockSpec(memory_space=pl.ANY)],
        out_specs=vmem,
        scratch_shapes=[
            pltpu.VMEM((4, KV_HEADS, 2 * HEAD_DIM, TOK // 4), jnp.bfloat16),
            pltpu.VMEM(inputs.shape, inputs.dtype),
            pltpu.SemaphoreType.DMA,
        ],
        compiler_params=pltpu.CompilerParams(vmem_limit_bytes=32 * 2**20),
        name="weight_products",
    )(place, *lines, inputs)


def other_core(x):
    return lax.ppermute(x, "ctx", [(i, i ^ 1) for i in range(CORES * RING)])


def from_z(x, away):
    return lax.ppermute(
        x, "ctx", [(((i // CORES + away) % RING) * CORES + i % CORES, i) for i in range(CORES * RING)]
    )


def other_of_pair(x):
    return lax.ppermute(x, "tp", [(i, i ^ 1) for i in range(SIDE * SIDE)])


def from_y(x, away):
    return lax.ppermute(
        x, "tp", [(((i // SIDE + away) % SIDE) * SIDE + i % SIDE, i) for i in range(SIDE * SIDE)]
    )


def from_x(x, away):
    return lax.ppermute(
        x, "tp", [(i // SIDE * SIDE + (i % SIDE + away) % SIDE, i) for i in range(SIDE * SIDE)]
    )


def gathered(x, hop):
    return [x] + [hop(x, away) for away in range(1, SIDE)]


def summed(x, hop):
    total = x
    for away in range(1, SIDE):
        total = total + hop(x, away)
    return total


def reduce_ctx(keep, arrived, rows):
    bf16, f32 = jnp.bfloat16, jnp.float32
    half = rows // 2

    def pair(away, low, high):
        kept = keep[away * rows + low : away * rows + high]
        return kept.astype(f32) + arrived[away][low:high].astype(f32)

    ahead, behind = lax.optimization_barrier(
        (pair(2, 0, half).astype(bf16), pair(2, half, rows).astype(bf16))
    )
    from_before, from_after = lax.optimization_barrier(
        (from_z(ahead, RING - 1), from_z(behind, 1))
    )
    up = jnp.concatenate([pair(1, 0, half) + from_before.astype(f32), pair(1, half, rows)], axis=0)
    down = jnp.concatenate([pair(3, 0, half), pair(3, half, rows) + from_after.astype(f32)], axis=0)
    up, down = lax.optimization_barrier((up.astype(bf16), down.astype(bf16)))
    arrived_up, arrived_down = lax.optimization_barrier((from_z(up, RING - 1), from_z(down, 1)))
    return pair(0, 0, rows) + arrived_up.astype(f32) + arrived_down.astype(f32)


def shards(
    query, keys, values, d_out, inputs, kv_weight, moment, velocity, doc_lengths, block_start
):
    ctx, tp = lax.axis_index("ctx"), lax.axis_index("tp")
    my_z, my_core = ctx // CORES, ctx % CORES
    head_at = (tp // 2) * HEAD_DIM
    wide = HEADS_IN * HEAD_DIM
    bf16, f32 = jnp.bfloat16, jnp.float32
    own_kv = jnp.concatenate(
        [
            lax.dynamic_slice_in_dim(keys, head_at, HEAD_DIM, 1),
            lax.dynamic_slice_in_dim(values, head_at, HEAD_DIM, 1),
        ],
        axis=1,
    )
    after, before = lax.optimization_barrier((from_z(own_kv, 1), from_z(own_kv, 3)))
    upper, lower = lax.optimization_barrier(
        (from_z(after[: TOK // 2], 1), from_z(before[TOK // 2 :], 3))
    )
    across = jnp.concatenate([upper, lower], axis=0)
    same_core = [own_kv, after, across, before]
    kv_pieces = same_core + [other_core(piece) for piece in same_core]

    def for_other_core(x):
        return other_core(lax.dynamic_slice_in_dim(x, (1 - my_core) * wide, wide, 1))

    dq_own, dq_other, keep, send = attention(
        doc_lengths,
        block_start,
        ctx.reshape(1),
        (query, for_other_core(query)),
        (d_out, for_other_core(d_out)),
        kv_pieces,
    )
    place = jnp.stack([my_z, my_core, tp // SIDE, tp % SIDE]).astype(jnp.int32)
    even = tp % 2 == 0
    arrived = other_core(send).reshape(RING, TOK, 2 * HEAD_DIM)
    gradient = reduce_ctx(keep, arrived, TOK)
    dq_back = other_core(dq_other)
    d_query = jnp.where(
        my_core == 0,
        jnp.concatenate([dq_own, dq_back], axis=1),
        jnp.concatenate([dq_back, dq_own], axis=1),
    )
    gradient, d_query = lax.optimization_barrier((gradient, d_query))
    upper, lower = gradient[: TOK // 2], gradient[TOK // 2 :]
    given = jnp.where(even, lower, upper).astype(bf16)
    kept = jnp.where(even, upper, lower)
    own_part = (kept + other_of_pair(given).astype(f32)).astype(bf16)
    quarter = TOK // 4
    line_y = jnp.stack(gathered(own_part[:quarter], from_y))
    line_x = jnp.stack(gathered(own_part[quarter:], from_x))
    line_y, line_x = lax.optimization_barrier((line_y, line_x))
    far_x, far_y, *near = lax.optimization_barrier(
        [from_x(line_y, 2), from_y(line_x, 2)]
        + [hop(line, away) for away in (1, 3) for line, hop in ((line_y, from_x), (line_x, from_y))]
    )
    along_x = [line_y, near[0], far_x, near[2]]
    along_y = [line_x, near[1], far_y, near[3]]
    features = inputs.shape[1]
    flat = (RING * 2 * HEAD_DIM, features)
    for_other = weight_products(1, place, along_x + along_y, inputs).reshape(flat)
    arrived = other_core(for_other)
    for_mine = weight_products(0, place, along_x + along_y, inputs).reshape(flat)
    weight_grad = reduce_ctx(for_mine, arrived.reshape(RING, 2 * HEAD_DIM, features), 2 * HEAD_DIM)
    new_moment = beta_one * moment + (1.0 - beta_one) * weight_grad
    new_velocity = beta_two * velocity + (1.0 - beta_two) * weight_grad * weight_grad
    direction = (
        new_moment / first_correction / (jnp.sqrt(new_velocity / second_correction) + adam_eps)
    )
    squares = jnp.stack(
        [jnp.sum(kv_weight * kv_weight, axis=1), jnp.sum(direction * direction, axis=1)]
    )
    weight_square, update_square = summed(summed(squares, from_y), from_x)
    trust_ratio = jnp.sqrt(weight_square) / jnp.sqrt(update_square + norm_eps)
    update = trust_ratio[:, None] * direction
    return (d_query, update, new_moment, new_velocity)


def solution(mesh):
    split = P("ctx", "tp")
    rows = P("ctx", None)
    return jax.shard_map(
        shards,
        mesh=mesh,
        in_specs=(split, rows, rows, split, split, split, split, split, P(), P()),
        out_specs=(split,) * 4,
        check_vma=False,
    )
```
